512 devices in a mesh: row: 16 (over y, core), col: 32 (over z, x).
Axes of the slice: x: 4, y: 8, z: 8, core: 2. Of those that a mesh axis runs over, the one named last changes fastest.
Arguments:
- amplitudes: float32 [2, 128, 1048576], P(None, 'row', 'col'), may hold values from -6 to 6
- qubit_order: int32 [11], replicated, may hold values from 0 to 10, each once
Outputs:
- correlators: float32 [32, 32768], P('col', 'row')
The draws below stay inside these ranges and needn't reach their ends.
Inputs may be any that keep to these rules, and one draw needn't show every extreme that they name: `qubit_order`: a permutation of 0 to 10.
All inputs are finite; a program needn't handle non-finite values.
Results may differ from the reference program's by a relative error of at most 0.0003.
Values sent between devices are 32-bit elements; how exact they have to be, the bound alone decides.
A program may use at most 64 MiB of HBM per device.

```python
import jax
import jax.numpy as jnp

MEASURED_QUBITS = 20
PERM_BITS = 11
UNMEASURED = 128
OUTCOMES = 1048576
SLICE = 32768


def shard_levels(key, dims, cuts, low, top_value):
    level, own = 1.0, jax.random.fold_in(key, 6)
    for position, blocks in cuts:
        heights = jnp.exp(jax.random.uniform(jax.random.fold_in(own, position), (blocks,), jnp.float32, low / len(cuts), top_value / len(cuts)))
        level = level * jnp.repeat(heights, dims[position] // blocks).reshape([-1 if axis == position else 1 for axis in range(len(dims))])
    return level


def bell_draw(own_key, extent, scale, reach, cuts=(), held_as=jnp.bfloat16):
    drawn = jax.random.normal(own_key, extent, jnp.float32) * scale
    if len(cuts) > 0:
        drawn = shard_levels(own_key, extent, cuts, -0.22, 0.18) * drawn
    return jnp.clip(drawn, min=-reach, max=reach).astype(held_as)


def setup_inputs(seed: int = 0) -> dict:
    key_list = jax.random.split(jax.random.key(seed), 3)
    amplitudes = bell_draw(key_list[0], (2, UNMEASURED, OUTCOMES), 1.0, 6.0, ((1, 16), (2, 32)), jnp.float32)
    qubit_order = jax.random.permutation(key_list[1], PERM_BITS).astype(jnp.int32)
    return {"amplitudes": amplitudes, "qubit_order": qubit_order}


def source_index(qubit_order):
    count = qubit_order.shape[0]
    target = jnp.arange(2 ** count, dtype=jnp.int32)
    source = jnp.zeros_like(target)
    for bit_location in range(count):
        bit_value = jnp.bitwise_and(jnp.right_shift(target, bit_location), 1)
        source = source + jnp.left_shift(bit_value, qubit_order[bit_location].astype(jnp.int32))
    return source.astype(jnp.int32)


def reference(amplitudes, qubit_order):
    marginal = jnp.sum(amplitudes * amplitudes, axis=(0, 1))
    probability_total = jnp.sum(marginal)
    perm_span = 2 ** qubit_order.shape[0]
    ordered = jnp.take(marginal.reshape(-1, perm_span), source_index(qubit_order), axis=1).reshape(-1)
    walsh_coefficients = ordered
    for bit_location in range(MEASURED_QUBITS):
        folded = walsh_coefficients.reshape(-1, 2, 2 ** bit_location)
        walsh_coefficients = jnp.stack([folded[:, 0] + folded[:, 1], folded[:, 0] - folded[:, 1]], axis=1).reshape(-1)
    correlators = walsh_coefficients * (2.0 ** (MEASURED_QUBITS / 2)) / probability_total
    return correlators.reshape(OUTCOMES // SLICE, SLICE)
```

```python
import functools
import itertools

import jax
import jax.numpy as jnp
from jax import lax
from jax.experimental import pallas as pl
from jax.experimental.pallas import tpu as pltpu
from jax.sharding import PartitionSpec as P

NY, NK, NZ, NX = 8, 2, 8, 4
CHUNK = 4096
LANES = 128
ROWS = 9
PAIR = "pair"


def hops(offset):
    dy, dk, dz, dx = offset
    dx = 1 if dx == PAIR else min(dx, NX - dx)
    return min(dy, NY - dy) + min(dz, NZ - dz) + dx


def far_first(offsets):
    return sorted((o for o in offsets if o != (0, 0, 0, 0)), key=lambda o: -hops(o))


TWIN = (0, 1, 0, 0)
FIRST = far_first(itertools.product(range(NY), (0,), (0,), (0, PAIR)))
SECOND = far_first(itertools.product((0,), (0,), range(NZ), range(NX)))
ALONG_Z = far_first(itertools.product((0,), (0,), range(NZ), (0,)))
ALONG_X = far_first(itertools.product((0,), (0,), (0,), range(NX)))
GREETED = far_first({o for o in FIRST if o != (0, 0, 0, PAIR)} | set(ALONG_Z) | set(ALONG_X) | {TWIN})


class Places:
    def __init__(self):
        row, col = lax.axis_index("row"), lax.axis_index("col")
        self.y, self.k = lax.div(row, 2), lax.rem(row, 2)
        self.z, self.x = lax.div(col, NX), lax.rem(col, NX)
        self.pair_bit = lax.rem(self.x, 2)
        self.ys = [self.y] + [lax.rem(self.y + i, NY) for i in range(1, NY)]
        self.zs = [self.z] + [lax.rem(self.z + i, NZ) for i in range(1, NZ)]
        self.xs = {i: lax.rem(self.x + i, NX) for i in range(1, NX)} | {0: self.x, PAIR: self.x + 1 - 2 * self.pair_bit}
        self.row = {(i, 0): self.ys[i] * NK + self.k for i in range(NY)} | {(0, 1): row + 1 - 2 * self.k}
        self.col = {(i, j): self.zs[i] * NX + self.xs[j] for i in range(NZ) for j in range(NX)}
        self.col[0, PAIR] = self.z * NX + self.xs[PAIR]

    def at(self, offset):
        dy, dk, dz, dx = offset
        return {
            "device_id": (self.row[dy, dk], self.col[dz, dx]),
            "device_id_type": pl.DeviceIdType.MESH,
        }


def sign(bit):
    return (1 - 2 * bit).astype(jnp.float32)


def rows_summed(squares, odd):
    for level in range(3):
        half = squares.shape[1] // 2
        low, high = squares[:, :half], squares[:, half:]
        there = odd[level][:, :half]
        step = 2**level
        squares = jnp.where(there, high, low) + pltpu.roll(jnp.where(there, low, high), 8 - step, 0)
    return squares


def row_walsh(values, row_ids):
    for level in range(3):
        step = 2**level
        up, down = pltpu.roll(values, 8 - step, 0), pltpu.roll(values, step, 0)
        values = jnp.where((row_ids >> level) & 1 == 1, down - values, values + up)
    return values


def walsh_matrix():
    common = lax.broadcasted_iota(jnp.int32, (LANES, LANES), 0) & lax.broadcasted_iota(jnp.int32, (LANES, LANES), 1)
    parity = common ^ (common >> 4)
    parity = parity ^ (parity >> 2)
    parity = (parity ^ (parity >> 1)) & 1
    return (1 - 2 * parity).astype(jnp.float32).astype(jnp.bfloat16)


def walsh_over_first(values):
    count, *rest = values.shape
    for step in (4, 2, 1):
        pairs = values.reshape(count // (2 * step), 2, step, *rest)
        low, high = pairs[:, 0], pairs[:, 1]
        values = jnp.stack([low + high, low - high], axis=1).reshape(count, *rest)
    return values


def wait_for(slots, count, semaphore):
    pltpu.make_async_copy(slots.at[pl.ds(0, count)], slots.at[pl.ds(0, count)], semaphore).wait()


def exchange(amplitudes, out, held, keep, give, got, send1, recv1, send2, recv2, load_sem, twin_sem, sem1, sem2, seen):
    here = Places()

    loads = []
    for part in range(NY):
        columns = pl.ds(part * CHUNK, CHUNK)
        loads.append(pltpu.make_async_copy(amplitudes.at[:, :, columns], held.at[:, :, columns], load_sem.at[part]))
    for load in loads:
        load.start()
    barrier = pltpu.get_barrier_semaphore()
    for offset in GREETED:
        pl.semaphore_signal(barrier, inc=1, **here.at(offset))

    row_ids = lax.broadcasted_iota(jnp.int32, (8, CHUNK // 4), 0)
    odd = [(row_ids >> level) & 1 == 1 for level in range(3)]
    core_sign = sign(here.k)
    mass = jnp.zeros((8, 2 * LANES), jnp.float32)
    for part in range(NY):
        loads[part].wait()
        real = held[0, :, part * CHUNK : (part + 1) * CHUNK]
        imag = held[1, :, part * CHUNK : (part + 1) * CHUNK]
        squares = real * real + imag * imag
        zero, one = rows_summed(squares[:, : CHUNK // 2], odd), rows_summed(squares[:, CHUNK // 2 :], odd)
        mass = mass + (zero + one)
        one = core_sign * one
        keep[part] = zero + one
        give[part] = zero - one
    give[NY] = mass

    pl.semaphore_wait(barrier, len(GREETED))
    for offset in ALONG_Z:
        pl.semaphore_signal(seen, inc=1, **here.at(offset))

    twin = pltpu.make_async_remote_copy(give, got, twin_sem.at[0], twin_sem.at[1], **here.at(TWIN))
    twin.start()
    twin.wait_recv()

    parts = walsh_over_first(keep[...] + got[0:NY])
    mass = mass + got[NY]
    mass = jnp.sum(mass[:, :LANES] + mass[:, LANES:], axis=0, keepdims=True)
    for half in range(2):
        send1[:, half, 0:8, :] = parts[:, :, half * LANES : (half + 1) * LANES]
    send1[:, :, 8:9, :] = jnp.broadcast_to(mass, (NY, 2, 1, LANES))
    slot = here.y * 2 + here.pair_bit
    for offset in FIRST:
        bit = 1 - here.pair_bit if offset[3] == PAIR else here.pair_bit
        pltpu.make_async_remote_copy(
            send1.at[here.ys[offset[0]], bit], recv1.at[slot], sem1.at[0], sem1.at[1], **here.at(offset)
        ).start()
    recv1[slot] = send1[here.y, here.pair_bit]
    wait_for(recv1, len(FIRST), sem1.at[1])

    sums = recv1[...].reshape(NY, 2, ROWS, LANES).sum(axis=0)
    total = sums[0] + sums[1]
    send2[0] = total
    send2[1, 0:8, :] = sums[0, 0:8] - sums[1, 0:8]
    send2[1, 8:9, :] = total[8:9]

    pl.semaphore_wait(seen, len(ALONG_Z))
    slot = here.z * NX + here.x
    bits = {dx: lax.rem(here.xs[dx], 2) for dx in range(NX)}
    for offset in SECOND:
        pltpu.make_async_remote_copy(
            send2.at[bits[offset[3]]], recv2.at[slot], sem2.at[0], sem2.at[1], **here.at(offset)
        ).start()
    recv2[slot] = send2[here.pair_bit]
    matrix = walsh_matrix()
    signs = [sign(lax.rem(lax.div(here.z, 2**level), 2)) for level in (2, 1, 0)] + [sign(lax.div(here.x, 2))]
    wait_for(recv2, len(SECOND), sem2.at[1])

    terms = recv2[...]
    masses = jnp.sum(terms[:, 8:9, :], axis=0)
    terms = terms[:, 0:8, :]
    for factor in signs:
        half = terms.shape[0] // 2
        terms = terms[:half] + factor * terms[half:]
    rows = row_ids[:, :LANES]
    values = jnp.concatenate(
        [
            row_walsh(terms[0] + terms[1], rows),
            row_walsh(terms[0] - terms[1], rows),
            jnp.broadcast_to(masses, (16, LANES)),
        ],
        axis=0,
    )
    high = values.astype(jnp.bfloat16)
    rest = values - high.astype(jnp.float32)
    middle = rest.astype(jnp.bfloat16)
    low = (rest - middle.astype(jnp.float32)).astype(jnp.bfloat16)
    product = jnp.dot(jnp.concatenate([high, middle, low], axis=0), matrix, preferred_element_type=jnp.float32)
    out[...] = product[0:24] + product[32:56] + product[64:88]
    twin.wait_send()
    wait_for(recv1, len(FIRST), sem1.at[0])
    wait_for(recv2, len(SECOND), sem2.at[0])


def reorder(order, values, out):
    target = lax.broadcasted_iota(jnp.int32, (16, LANES), 0) * LANES + lax.broadcasted_iota(jnp.int32, (16, LANES), 1)
    source = jnp.zeros_like(target)
    for location in range(11):
        source = source + (((target >> location) & 1) << order[location])
    lane, row = source & 127, source >> 7
    row = ((row & 1) << 3) | ((row >> 3) & 1) | ((row >> 1) & 2) | ((row << 1) & 4)
    result = jnp.zeros((16, LANES), jnp.float32)
    for i in range(16):
        line = jnp.broadcast_to(values[i : i + 1, :], (16, LANES))
        result = jnp.where(row == i, jnp.take_along_axis(line, lane, axis=1), result)
    total = jnp.broadcast_to(values[16:17, 0:1], (16, LANES))
    out[...] = result * 2048.0 / total


def local(amplitudes, qubit_order):
    vmem = pl.BlockSpec(memory_space=pltpu.VMEM)
    f32 = jnp.float32
    values = pl.pallas_call(
        exchange,
        out_shape=jax.ShapeDtypeStruct((24, LANES), f32),
        in_specs=[pl.BlockSpec(memory_space=pl.ANY)],
        out_specs=vmem,
        scratch_shapes=[
            pltpu.VMEM((2, 8, NY * CHUNK), f32),
            pltpu.VMEM((NY, 8, 2 * LANES), f32),
            pltpu.VMEM((NY + 1, 8, 2 * LANES), f32),
            pltpu.VMEM((NY + 1, 8, 2 * LANES), f32),
            pltpu.VMEM((NY, 2, ROWS, LANES), f32),
            pltpu.VMEM((2 * NY, ROWS, LANES), f32),
            pltpu.VMEM((2, ROWS, LANES), f32),
            pltpu.VMEM((NZ * NX, ROWS, LANES), f32),
            pltpu.SemaphoreType.DMA((NY,)),
            pltpu.SemaphoreType.DMA((2,)),
            pltpu.SemaphoreType.DMA((2,)),
            pltpu.SemaphoreType.DMA((2,)),
            pltpu.SemaphoreType.REGULAR,
        ],
        compiler_params=pltpu.CompilerParams(
            collective_id=0, has_side_effects=True, vmem_limit_bytes=56 * 2**20
        ),
    )(amplitudes)
    result = pl.pallas_call(
        reorder,
        out_shape=jax.ShapeDtypeStruct((16, LANES), f32),
        in_specs=[pl.BlockSpec(memory_space=pltpu.SMEM), vmem],
        out_specs=vmem,
    )(qubit_order, values)
    return result.reshape(1, -1)


def solution(mesh):
    return jax.shard_map(
        local, mesh=mesh, in_specs=(P(None, "row", "col"), P()), out_specs=P("col", "row"), check_vma=False
    )
```

```python
import functools
import itertools

import jax
import jax.numpy as jnp
from jax import lax
from jax.experimental import pallas as pl
from jax.experimental.pallas import tpu as pltpu
from jax.sharding import PartitionSpec as P

NY, NK, NZ, NX = 8, 2, 8, 4
CHUNK = 4096
LANES = 128
ROWS = 9
PAIR = "pair"


def hops(offset):
    dy, dk, dz, dx = offset
    dx = 1 if dx == PAIR else min(dx, NX - dx)
    return min(dy, NY - dy) + min(dz, NZ - dz) + dx


def far_first(offsets):
    return sorted((o for o in offsets if o != (0, 0, 0, 0)), key=lambda o: -hops(o))


TWIN = (0, 1, 0, 0)
FAR_Y = (4,)
FAR = far_first(itertools.product(FAR_Y, range(NK), (0,), (0, PAIR)))
NEAR = far_first(o for o in itertools.product(range(NY), (0,), (0,), (0, PAIR)) if o[0] not in FAR_Y)
SLOTS = sorted(FAR + NEAR, key=lambda o: o[3] == PAIR)
OWN_SIDE = sum(o[3] != PAIR for o in SLOTS)
SECOND = far_first(itertools.product((0,), (0,), range(NZ), range(NX)))
NEXT_Z = [(0, 0, 1, 0), (0, 0, NZ - 1, 0)]
SECOND_Z = [(0, 0, 2, 0), (0, 0, NZ - 2, 0)]
ALONG_X = far_first(itertools.product((0,), (0,), (0,), range(NX)))
GREETED = far_first({o for o in FAR + NEAR if o != (0, 0, 0, PAIR)} | set(NEXT_Z) | set(ALONG_X) | {TWIN})


class Places:
    def __init__(self):
        row, col = lax.axis_index("row"), lax.axis_index("col")
        self.y, self.k = lax.div(row, 2), lax.rem(row, 2)
        self.z, self.x = lax.div(col, NX), lax.rem(col, NX)
        self.pair_bit = lax.rem(self.x, 2)
        self.ys = [self.y] + [lax.rem(self.y + i, NY) for i in range(1, NY)]
        self.zs = [self.z] + [lax.rem(self.z + i, NZ) for i in range(1, NZ)]
        self.xs = {i: lax.rem(self.x + i, NX) for i in range(1, NX)} | {0: self.x, PAIR: self.x + 1 - 2 * self.pair_bit}
        other = 1 - self.k
        self.row = {(i, j): self.ys[i] * NK + (other if j else self.k) for i in range(NY) for j in range(NK)}
        self.col = {(i, j): self.zs[i] * NX + self.xs[j] for i in range(NZ) for j in range(NX)}
        self.col[0, PAIR] = self.z * NX + self.xs[PAIR]

    def at(self, offset):
        dy, dk, dz, dx = offset
        return {
            "device_id": (self.row[dy, dk], self.col[dz, dx]),
            "device_id_type": pl.DeviceIdType.MESH,
        }


def sign(bit):
    return (1 - 2 * bit).astype(jnp.float32)


def rows_summed(squares, odd):
    for level in range(3):
        half = squares.shape[1] // 2
        low, high = squares[:, :half], squares[:, half:]
        there = odd[level][:, :half]
        step = 2**level
        squares = jnp.where(there, high, low) + pltpu.roll(jnp.where(there, low, high), 8 - step, 0)
    return squares


def row_walsh(values, row_ids):
    for level in range(3):
        step = 2**level
        up, down = pltpu.roll(values, 8 - step, 0), pltpu.roll(values, step, 0)
        values = jnp.where((row_ids >> level) & 1 == 1, down - values, values + up)
    return values


def walsh_matrix():
    common = lax.broadcasted_iota(jnp.int32, (LANES, LANES), 0) & lax.broadcasted_iota(jnp.int32, (LANES, LANES), 1)
    parity = common ^ (common >> 4)
    parity = parity ^ (parity >> 2)
    parity = (parity ^ (parity >> 1)) & 1
    return (1 - 2 * parity).astype(jnp.float32).astype(jnp.bfloat16)


def walsh_over_first(values):
    count, *rest = values.shape
    for step in (4, 2, 1):
        pairs = values.reshape(count // (2 * step), 2, step, *rest)
        low, high = pairs[:, 0], pairs[:, 1]
        values = jnp.stack([low + high, low - high], axis=1).reshape(count, *rest)
    return values


def wait_for(slots, count, semaphore):
    pltpu.make_async_copy(slots.at[pl.ds(0, count)], slots.at[pl.ds(0, count)], semaphore).wait()


def exchange(
    amplitudes, qubit_order, out, lanes, lines,
    held, order, keep, give, got, own, sent, recv1, send2, recv2, load_sem, order_sem, twin_sem, far_sem, near_sem, sem2, seen,
):
    here = Places()

    loads = []
    for part in range(NY):
        columns = pl.ds(part * CHUNK, CHUNK)
        loads.append(pltpu.make_async_copy(amplitudes.at[:, :, columns], held.at[:, :, columns], load_sem.at[part]))
    for load in loads:
        load.start()
    order_load = pltpu.make_async_copy(qubit_order, order, order_sem)
    order_load.start()
    barrier = pltpu.get_barrier_semaphore()
    for offset in GREETED:
        pl.semaphore_signal(barrier, inc=1, **here.at(offset))

    row_ids = lax.broadcasted_iota(jnp.int32, (8, CHUNK // 4), 0)
    odd = [(row_ids >> level) & 1 == 1 for level in range(3)]
    core_sign = sign(here.k)
    mass = jnp.zeros((8, 2 * LANES), jnp.float32)
    for part in range(NY):
        loads[part].wait()
        real = held[0, :, part * CHUNK : (part + 1) * CHUNK]
        imag = held[1, :, part * CHUNK : (part + 1) * CHUNK]
        squares = real * real + imag * imag
        zero, one = rows_summed(squares[:, : CHUNK // 2], odd), rows_summed(squares[:, CHUNK // 2 :], odd)
        mass = mass + (zero + one)
        one = core_sign * one
        keep[part] = zero + one
        give[part] = zero - one
    own_part, other_part = walsh_over_first(keep[...]), walsh_over_first(give[0:NY])
    give[0:NY] = other_part
    give[NY] = mass
    own_mass = jnp.sum(mass[:, :LANES] + mass[:, LANES:], axis=0, keepdims=True)
    spread = jnp.broadcast_to(own_mass, (NY, 1, LANES))
    for which, part in enumerate((own_part, other_part)):
        for half in range(2):
            own[which, half, :, 0:8, :] = part[:, :, half * LANES : (half + 1) * LANES]
            own[which, half, :, 8:9, :] = spread

    pl.semaphore_wait(barrier, len(GREETED))
    twin = pltpu.make_async_remote_copy(give, got, twin_sem.at[0], twin_sem.at[1], **here.at(TWIN))
    twin.start()
    sides = {0: here.pair_bit, PAIR: 1 - here.pair_bit}
    for offset in FAR:
        pltpu.make_async_remote_copy(
            own.at[offset[1], sides[offset[3]], here.ys[offset[0]]],
            recv1.at[SLOTS.index(offset)], far_sem.at[0], far_sem.at[1], **here.at(offset)
        ).start()
    for offset in NEXT_Z:
        pl.semaphore_signal(seen.at[0], inc=1, **here.at(offset))
    twin.wait_recv()

    mass = own_mass + jnp.sum(got[NY, :, :LANES] + got[NY, :, LANES:], axis=0, keepdims=True)
    spread = jnp.broadcast_to(mass, (NY, 1, LANES))
    for half in range(2):
        columns = slice(half * LANES, (half + 1) * LANES)
        sent[half, :, 0:8, :] = own[0, half, :, 0:8, :] + got[0:NY, :, columns]
        sent[half, :, 8:9, :] = spread
    for offset in NEAR:
        pltpu.make_async_remote_copy(
            sent.at[sides[offset[3]], here.ys[offset[0]]],
            recv1.at[SLOTS.index(offset)], near_sem.at[0], near_sem.at[1], **here.at(offset)
        ).start()

    pl.semaphore_wait(seen.at[0], len(NEXT_Z))
    for offset in SECOND_Z:
        pl.semaphore_signal(seen.at[1], inc=1, **here.at(offset))
    order_load.wait()
    lanes[...], lines[...] = sources(order)
    matrix = walsh_matrix()
    signs = [sign(lax.rem(lax.div(here.z, 2**level), 2)) for level in (2, 1, 0)] + [sign(lax.div(here.x, 2))]
    pair_sign = sign(here.pair_bit)
    pl.semaphore_wait(seen.at[1], len(SECOND_Z))
    for offset in ALONG_X:
        pl.semaphore_signal(seen.at[2], inc=1, **here.at(offset))
    pl.semaphore_wait(seen.at[2], len(ALONG_X))
    wait_for(recv1, len(FAR), far_sem.at[1])
    wait_for(recv1, len(NEAR), near_sem.at[1])

    this_side = recv1[0:OWN_SIDE].sum(axis=0) + sent[here.pair_bit, here.y]
    that_side = recv1[OWN_SIDE:].sum(axis=0)
    send2[0] = this_side + that_side
    send2[1, 0:8, :] = pair_sign * (this_side[0:8] - that_side[0:8])
    send2[1, 8:9, :] = this_side[8:9] + that_side[8:9]

    slot = here.z * NX + here.x
    bits = {dx: lax.rem(here.xs[dx], 2) for dx in range(NX)}
    for offset in SECOND:
        with_mass = offset[3] % 2 == 0
        height, pair = (pl.ds(0, ROWS), 0) if with_mass else (pl.ds(0, 8), 2)
        pltpu.make_async_remote_copy(
            send2.at[bits[offset[3]], height], recv2.at[slot, height], sem2.at[pair], sem2.at[pair + 1], **here.at(offset)
        ).start()
    recv2[slot] = send2[here.pair_bit]
    light = recv2.at[pl.ds(0, NZ * NX // 2), pl.ds(0, 8)]
    wait_for(recv2, NZ * NX // 2 - 1, sem2.at[1])
    pltpu.make_async_copy(light, light, sem2.at[3]).wait()

    masses = functools.reduce(jnp.add, [recv2[2 * i + here.pair_bit, 8:9, :] for i in range(NZ * NX // 2)])
    terms = recv2[:, 0:8, :]
    for factor in signs:
        half = terms.shape[0] // 2
        terms = terms[:half] + factor * terms[half:]
    rows = row_ids[:, :LANES]
    values = jnp.concatenate(
        [
            row_walsh(terms[0] + terms[1], rows),
            row_walsh(terms[0] - terms[1], rows),
            jnp.broadcast_to(masses, (16, LANES)),
        ],
        axis=0,
    )
    high = values.astype(jnp.bfloat16)
    rest = values - high.astype(jnp.float32)
    middle = rest.astype(jnp.bfloat16)
    low = (rest - middle.astype(jnp.float32)).astype(jnp.bfloat16)
    product = jnp.dot(jnp.concatenate([high, middle, low], axis=0), matrix, preferred_element_type=jnp.float32)
    out[...] = product[0:24] + product[32:56] + product[64:88]
    twin.wait_send()
    wait_for(recv1, len(FAR), far_sem.at[0])
    wait_for(recv1, len(NEAR), near_sem.at[0])
    wait_for(recv2, NZ * NX // 2 - 1, sem2.at[0])
    pltpu.make_async_copy(light, light, sem2.at[2]).wait()


def sources(order):
    target = lax.broadcasted_iota(jnp.int32, (16, LANES), 0) * LANES + lax.broadcasted_iota(jnp.int32, (16, LANES), 1)
    source = jnp.zeros_like(target)
    for location in range(11):
        source = source + (((target >> location) & 1) << order[location])
    row = source >> 7
    return source & 127, ((row & 1) << 3) | ((row >> 3) & 1) | ((row >> 1) & 2) | ((row << 1) & 4)


def reorder(values, lanes, lines, out):
    lane, line = lanes[...], lines[...]
    result = jnp.zeros((16, LANES), jnp.float32)
    for i in range(16):
        row = jnp.broadcast_to(values[i : i + 1, :], (16, LANES))
        result = jnp.where(line == i, jnp.take_along_axis(row, lane, axis=1), result)
    total = jnp.broadcast_to(values[16:17, 0:1], (16, LANES))
    out[...] = result * 1024.0 / total


def local(amplitudes, qubit_order):
    vmem = pl.BlockSpec(memory_space=pltpu.VMEM)
    f32 = jnp.float32
    tables = pl.pallas_call(
        exchange,
        out_shape=[pltpu.VMEM((24, LANES), f32), pltpu.VMEM((16, LANES), jnp.int32), pltpu.VMEM((16, LANES), jnp.int32)],
        in_specs=[pl.BlockSpec(memory_space=pl.ANY), pl.BlockSpec(memory_space=pl.ANY)],
        out_specs=[vmem] * 3,
        scratch_shapes=[
            pltpu.VMEM((2, 8, NY * CHUNK), f32),
            pltpu.SMEM((11,), jnp.int32),
            pltpu.VMEM((NY, 8, 2 * LANES), f32),
            pltpu.VMEM((NY + 1, 8, 2 * LANES), f32),
            pltpu.VMEM((NY + 1, 8, 2 * LANES), f32),
            pltpu.VMEM((NK, 2, NY, ROWS, LANES), f32),
            pltpu.VMEM((2, NY, ROWS, LANES), f32),
            pltpu.VMEM((len(SLOTS), ROWS, LANES), f32),
            pltpu.VMEM((2, ROWS, LANES), f32),
            pltpu.VMEM((NZ * NX, ROWS, LANES), f32),
            pltpu.SemaphoreType.DMA((NY,)),
            pltpu.SemaphoreType.DMA,
            pltpu.SemaphoreType.DMA((2,)),
            pltpu.SemaphoreType.DMA((2,)),
            pltpu.SemaphoreType.DMA((2,)),
            pltpu.SemaphoreType.DMA((4,)),
            pltpu.SemaphoreType.REGULAR((3,)),
        ],
        compiler_params=pltpu.CompilerParams(
            collective_id=0, has_side_effects=True, vmem_limit_bytes=56 * 2**20
        ),
    )(amplitudes, qubit_order)
    result = pl.pallas_call(
        reorder,
        out_shape=jax.ShapeDtypeStruct((16, LANES), f32),
        in_specs=[vmem] * 3,
        out_specs=vmem,
    )(*(pltpu.with_memory_space_constraint(table, pltpu.VMEM) for table in tables))
    return result.reshape(1, -1)


def solution(mesh):
    return jax.shard_map(
        local, mesh=mesh, in_specs=(P(None, "row", "col"), P()), out_specs=P("col", "row"), check_vma=False
    )
```

```python
import functools
import itertools

import jax
import jax.numpy as jnp
from jax import lax
from jax.experimental import pallas as pl
from jax.experimental.pallas import tpu as pltpu
from jax.sharding import PartitionSpec as P

NY, NK, NZ, NX = 8, 2, 8, 4
CHUNK = 4096
LANES = 128
ROWS = 9
PAIR = "pair"


def hops(offset):
    dy, dk, dz, dx = offset
    dx = 1 if dx == PAIR else min(dx, NX - dx)
    return min(dy, NY - dy) + min(dz, NZ - dz) + dx


def far_first(offsets):
    return sorted((o for o in offsets if o != (0, 0, 0, 0)), key=lambda o: -hops(o))


TWIN = (0, 1, 0, 0)
FAR_Y = (4,)
FAR = far_first(itertools.product(FAR_Y, range(NK), (0,), (0, PAIR)))
NEAR = far_first(o for o in itertools.product(range(NY), (0,), (0,), (0, PAIR)) if o[0] not in FAR_Y)
SLOTS = sorted(FAR + NEAR, key=lambda o: o[3] == PAIR)
OWN_SIDE = sum(o[3] != PAIR for o in SLOTS)
ALONG_X = far_first(itertools.product((0,), (0,), (0,), range(NX)))
GREETED = far_first({o for o in FAR + NEAR if o != (0, 0, 0, PAIR)} | set(ALONG_X) | {TWIN})


class Places:
    def __init__(self):
        row, col = lax.axis_index("row"), lax.axis_index("col")
        self.y, self.k = lax.div(row, 2), lax.rem(row, 2)
        self.z, self.x = lax.div(col, NX), lax.rem(col, NX)
        self.pair_bit = lax.rem(self.x, 2)
        self.ys = [self.y] + [lax.rem(self.y + i, NY) for i in range(1, NY)]
        self.zs = [self.z] + [lax.rem(self.z + i, NZ) for i in range(1, NZ)]
        self.xs = {i: lax.rem(self.x + i, NX) for i in range(1, NX)} | {0: self.x, PAIR: self.x + 1 - 2 * self.pair_bit}
        other = 1 - self.k
        self.row = {(i, j): self.ys[i] * NK + (other if j else self.k) for i in range(NY) for j in range(NK)}
        self.col = {(i, j): self.zs[i] * NX + self.xs[j] for i in range(NZ) for j in range(NX)}
        self.col[0, PAIR] = self.z * NX + self.xs[PAIR]

    def at_z(self, z, dx=0):
        return {
            "device_id": (self.row[0, 0], z * NX + self.xs[dx]),
            "device_id_type": pl.DeviceIdType.MESH,
        }

    def at(self, offset):
        dy, dk, dz, dx = offset
        return {
            "device_id": (self.row[dy, dk], self.col[dz, dx]),
            "device_id_type": pl.DeviceIdType.MESH,
        }


def sign(bit):
    return (1 - 2 * bit).astype(jnp.float32)


def rows_summed(squares, odd):
    for level in range(3):
        half = squares.shape[1] // 2
        low, high = squares[:, :half], squares[:, half:]
        there = odd[level][:, :half]
        step = 2**level
        squares = jnp.where(there, high, low) + pltpu.roll(jnp.where(there, low, high), 8 - step, 0)
    return squares


def row_walsh(values, row_ids):
    for level in range(3):
        step = 2**level
        up, down = pltpu.roll(values, 8 - step, 0), pltpu.roll(values, step, 0)
        values = jnp.where((row_ids >> level) & 1 == 1, down - values, values + up)
    return values


def walsh_matrix():
    common = lax.broadcasted_iota(jnp.int32, (LANES, LANES), 0) & lax.broadcasted_iota(jnp.int32, (LANES, LANES), 1)
    parity = common ^ (common >> 4)
    parity = parity ^ (parity >> 2)
    parity = (parity ^ (parity >> 1)) & 1
    return (1 - 2 * parity).astype(jnp.float32).astype(jnp.bfloat16)


def walsh_over_first(values):
    count, *rest = values.shape
    for step in (4, 2, 1):
        pairs = values.reshape(count // (2 * step), 2, step, *rest)
        low, high = pairs[:, 0], pairs[:, 1]
        values = jnp.stack([low + high, low - high], axis=1).reshape(count, *rest)
    return values


def wait_for(slots, count, semaphore):
    pltpu.make_async_copy(slots.at[pl.ds(0, count)], slots.at[pl.ds(0, count)], semaphore).wait()


def exchange(
    amplitudes, qubit_order, out, lanes, lines,
    held, order, keep, give, got, own, sent, recv1, send2, recv2, load_sem, order_sem, twin_sem, far_sem, near_sem, sem2, seen,
):
    here = Places()

    loads = []
    for part in range(NY):
        columns = pl.ds(part * CHUNK, CHUNK)
        loads.append(pltpu.make_async_copy(amplitudes.at[:, :, columns], held.at[:, :, columns], load_sem.at[part]))
    for load in loads:
        load.start()
    order_load = pltpu.make_async_copy(qubit_order, order, order_sem)
    order_load.start()
    barrier = pltpu.get_barrier_semaphore()
    for offset in GREETED:
        pl.semaphore_signal(barrier, inc=1, **here.at(offset))
    for z in range(NZ - 1, 0, -1):
        @pl.when(z > here.z)
        def _():
            pl.semaphore_signal(barrier, inc=1, **here.at_z(z))

    row_ids = lax.broadcasted_iota(jnp.int32, (8, CHUNK // 4), 0)
    odd = [(row_ids >> level) & 1 == 1 for level in range(3)]
    core_sign = sign(here.k)
    mass = jnp.zeros((8, 2 * LANES), jnp.float32)
    for part in range(NY):
        loads[part].wait()
        real = held[0, :, part * CHUNK : (part + 1) * CHUNK]
        imag = held[1, :, part * CHUNK : (part + 1) * CHUNK]
        squares = real * real + imag * imag
        zero, one = rows_summed(squares[:, : CHUNK // 2], odd), rows_summed(squares[:, CHUNK // 2 :], odd)
        mass = mass + (zero + one)
        one = core_sign * one
        keep[part] = zero + one
        give[part] = zero - one
    own_part, other_part = walsh_over_first(keep[...]), walsh_over_first(give[0:NY])
    give[0:NY] = other_part
    give[NY] = mass
    own_mass = jnp.sum(mass[:, :LANES] + mass[:, LANES:], axis=0, keepdims=True)
    spread = jnp.broadcast_to(own_mass, (NY, 1, LANES))
    for which, part in enumerate((own_part, other_part)):
        for half in range(2):
            own[which, half, :, 0:8, :] = part[:, :, half * LANES : (half + 1) * LANES]
            own[which, half, :, 8:9, :] = spread

    pl.semaphore_wait(barrier, len(GREETED) + here.z)
    twin = pltpu.make_async_remote_copy(give, got, twin_sem.at[0], twin_sem.at[1], **here.at(TWIN))
    twin.start()
    sides = {0: here.pair_bit, PAIR: 1 - here.pair_bit}
    for offset in FAR:
        pltpu.make_async_remote_copy(
            own.at[offset[1], sides[offset[3]], here.ys[offset[0]]],
            recv1.at[SLOTS.index(offset)], far_sem.at[0], far_sem.at[1], **here.at(offset)
        ).start()
    for offset in ALONG_X:
        pl.semaphore_signal(seen.at[0], inc=1, **here.at(offset))
    for z in range(NZ - 1):
        @pl.when(z < here.z)
        def _():
            pl.semaphore_signal(seen.at[1], inc=1, **here.at_z(z))
    twin.wait_recv()

    mass = own_mass + jnp.sum(got[NY, :, :LANES] + got[NY, :, LANES:], axis=0, keepdims=True)
    spread = jnp.broadcast_to(mass, (NY, 1, LANES))
    for half in range(2):
        columns = slice(half * LANES, (half + 1) * LANES)
        sent[half, :, 0:8, :] = own[0, half, :, 0:8, :] + got[0:NY, :, columns]
        sent[half, :, 8:9, :] = spread
    for offset in NEAR:
        pltpu.make_async_remote_copy(
            sent.at[sides[offset[3]], here.ys[offset[0]]],
            recv1.at[SLOTS.index(offset)], near_sem.at[0], near_sem.at[1], **here.at(offset)
        ).start()

    order_load.wait()
    lanes[...], lines[...] = sources(order)
    matrix = walsh_matrix()
    signs = [sign(lax.rem(lax.div(here.z, 2**level), 2)) for level in (2, 1, 0)] + [sign(lax.div(here.x, 2))]
    pair_sign = sign(here.pair_bit)
    wait_for(recv1, len(FAR), far_sem.at[1])
    wait_for(recv1, len(NEAR), near_sem.at[1])

    this_side = recv1[0:OWN_SIDE].sum(axis=0) + sent[here.pair_bit, here.y]
    that_side = recv1[OWN_SIDE:].sum(axis=0)
    send2[0] = this_side + that_side
    send2[1, 0:8, :] = pair_sign * (this_side[0:8] - that_side[0:8])
    send2[1, 8:9, :] = this_side[8:9] + that_side[8:9]

    pl.semaphore_wait(seen.at[0], len(ALONG_X))
    slot = here.z * NX + here.x
    bits = {dx: lax.rem(here.xs[dx], 2) for dx in range(NX)}
    for z in range(NZ):
        if z:
            @pl.when(here.z == z - 1)
            def _():
                pl.semaphore_wait(seen.at[1], NZ - z)
        for dx in (2, 1, 3, 0):
            height, pair = (pl.ds(0, ROWS), 0) if dx % 2 == 0 else (pl.ds(0, 8), 2)
            copy = pltpu.make_async_remote_copy(
                send2.at[bits[dx], height], recv2.at[slot, height], sem2.at[pair], sem2.at[pair + 1], **here.at_z(z, dx)
            )
            if dx:
                copy.start()
            else:
                pl.when(here.z != z)(copy.start)
    recv2[slot] = send2[here.pair_bit]
    light = recv2.at[pl.ds(0, NZ * NX // 2), pl.ds(0, 8)]
    wait_for(recv2, NZ * NX // 2 - 1, sem2.at[1])
    pltpu.make_async_copy(light, light, sem2.at[3]).wait()

    masses = functools.reduce(jnp.add, [recv2[2 * i + here.pair_bit, 8:9, :] for i in range(NZ * NX // 2)])
    terms = recv2[:, 0:8, :]
    for factor in signs:
        half = terms.shape[0] // 2
        terms = terms[:half] + factor * terms[half:]
    rows = row_ids[:, :LANES]
    values = jnp.concatenate(
        [
            row_walsh(terms[0] + terms[1], rows),
            row_walsh(terms[0] - terms[1], rows),
            jnp.broadcast_to(masses, (16, LANES)),
        ],
        axis=0,
    )
    high = values.astype(jnp.bfloat16)
    rest = values - high.astype(jnp.float32)
    middle = rest.astype(jnp.bfloat16)
    low = (rest - middle.astype(jnp.float32)).astype(jnp.bfloat16)
    product = jnp.dot(jnp.concatenate([high, middle, low], axis=0), matrix, preferred_element_type=jnp.float32)
    out[...] = product[0:24] + product[32:56] + product[64:88]
    twin.wait_send()
    wait_for(recv1, len(FAR), far_sem.at[0])
    wait_for(recv1, len(NEAR), near_sem.at[0])
    wait_for(recv2, NZ * NX // 2 - 1, sem2.at[0])
    pltpu.make_async_copy(light, light, sem2.at[2]).wait()


def sources(order):
    target = lax.broadcasted_iota(jnp.int32, (16, LANES), 0) * LANES + lax.broadcasted_iota(jnp.int32, (16, LANES), 1)
    source = jnp.zeros_like(target)
    for location in range(11):
        source = source + (((target >> location) & 1) << order[location])
    row = source >> 7
    return source & 127, ((row & 1) << 3) | ((row >> 3) & 1) | ((row >> 1) & 2) | ((row << 1) & 4)


def reorder(values, lanes, lines, out):
    lane, line = lanes[...], lines[...]
    result = jnp.zeros((16, LANES), jnp.float32)
    for i in range(16):
        row = jnp.broadcast_to(values[i : i + 1, :], (16, LANES))
        result = jnp.where(line == i, jnp.take_along_axis(row, lane, axis=1), result)
    total = jnp.broadcast_to(values[16:17, 0:1], (16, LANES))
    out[...] = result * 1024.0 / total


def local(amplitudes, qubit_order):
    vmem = pl.BlockSpec(memory_space=pltpu.VMEM)
    f32 = jnp.float32
    tables = pl.pallas_call(
        exchange,
        out_shape=[pltpu.VMEM((24, LANES), f32), pltpu.VMEM((16, LANES), jnp.int32), pltpu.VMEM((16, LANES), jnp.int32)],
        in_specs=[pl.BlockSpec(memory_space=pl.ANY), pl.BlockSpec(memory_space=pl.ANY)],
        out_specs=[vmem] * 3,
        scratch_shapes=[
            pltpu.VMEM((2, 8, NY * CHUNK), f32),
            pltpu.SMEM((11,), jnp.int32),
            pltpu.VMEM((NY, 8, 2 * LANES), f32),
            pltpu.VMEM((NY + 1, 8, 2 * LANES), f32),
            pltpu.VMEM((NY + 1, 8, 2 * LANES), f32),
            pltpu.VMEM((NK, 2, NY, ROWS, LANES), f32),
            pltpu.VMEM((2, NY, ROWS, LANES), f32),
            pltpu.VMEM((len(SLOTS), ROWS, LANES), f32),
            pltpu.VMEM((2, ROWS, LANES), f32),
            pltpu.VMEM((NZ * NX, ROWS, LANES), f32),
            pltpu.SemaphoreType.DMA((NY,)),
            pltpu.SemaphoreType.DMA,
            pltpu.SemaphoreType.DMA((2,)),
            pltpu.SemaphoreType.DMA((2,)),
            pltpu.SemaphoreType.DMA((2,)),
            pltpu.SemaphoreType.DMA((4,)),
            pltpu.SemaphoreType.REGULAR((2,)),
        ],
        compiler_params=pltpu.CompilerParams(
            collective_id=0, has_side_effects=True, vmem_limit_bytes=56 * 2**20
        ),
    )(amplitudes, qubit_order)
    result = pl.pallas_call(
        reorder,
        out_shape=jax.ShapeDtypeStruct((16, LANES), f32),
        in_specs=[vmem] * 3,
        out_specs=vmem,
    )(*(pltpu.with_memory_space_constraint(table, pltpu.VMEM) for table in tables))
    return result.reshape(1, -1)


def solution(mesh):
    return jax.shard_map(
        local, mesh=mesh, in_specs=(P(None, "row", "col"), P()), out_specs=P("col", "row"), check_vma=False
    )
```

```python
import functools
import itertools

import jax
import jax.numpy as jnp
from jax import lax
from jax.experimental import pallas as pl
from jax.experimental.pallas import tpu as pltpu
from jax.sharding import PartitionSpec as P

NY, NK, NZ, NX = 8, 2, 8, 4
CHUNK = 4096
LANES = 128
ROWS = 9
PAIR = "pair"


def hops(offset):
    dy, dk, dz, dx = offset
    dx = 1 if dx == PAIR else min(dx, NX - dx)
    return min(dy, NY - dy) + min(dz, NZ - dz) + dx


def far_first(offsets):
    return sorted((o for o in offsets if o != (0, 0, 0, 0)), key=lambda o: -hops(o))


TWIN = (0, 1, 0, 0)
FAR_Y = (4,)
FAR = far_first(itertools.product(FAR_Y, range(NK), (0,), (0, PAIR)))
NEAR = far_first(o for o in itertools.product(range(NY), (0,), (0,), (0, PAIR)) if o[0] not in FAR_Y)
SLOTS = sorted(FAR + NEAR, key=lambda o: o[3] == PAIR)
OWN_SIDE = sum(o[3] != PAIR for o in SLOTS)
ALONG_X = far_first(itertools.product((0,), (0,), (0,), range(NX)))
GREETED = far_first({o for o in FAR + NEAR if o != (0, 0, 0, PAIR)} | set(ALONG_X) | {TWIN})


class Places:
    def __init__(self):
        row, col = lax.axis_index("row"), lax.axis_index("col")
        self.y, self.k = lax.div(row, 2), lax.rem(row, 2)
        self.z, self.x = lax.div(col, NX), lax.rem(col, NX)
        self.pair_bit = lax.rem(self.x, 2)
        self.ys = [self.y] + [lax.rem(self.y + i, NY) for i in range(1, NY)]
        self.zs = [self.z] + [lax.rem(self.z + i, NZ) for i in range(1, NZ)]
        self.xs = {i: lax.rem(self.x + i, NX) for i in range(1, NX)} | {0: self.x, PAIR: self.x + 1 - 2 * self.pair_bit}
        other = 1 - self.k
        self.row = {(i, j): self.ys[i] * NK + (other if j else self.k) for i in range(NY) for j in range(NK)}
        self.col = {(i, j): self.zs[i] * NX + self.xs[j] for i in range(NZ) for j in range(NX)}
        self.col[0, PAIR] = self.z * NX + self.xs[PAIR]

    def at_z(self, z, dx=0):
        return {
            "device_id": (self.row[0, 0], z * NX + self.xs[dx]),
            "device_id_type": pl.DeviceIdType.MESH,
        }

    def at(self, offset):
        dy, dk, dz, dx = offset
        return {
            "device_id": (self.row[dy, dk], self.col[dz, dx]),
            "device_id_type": pl.DeviceIdType.MESH,
        }


def sign(bit):
    return (1 - 2 * bit).astype(jnp.float32)


def rows_summed(squares, odd):
    for level in range(3):
        half = squares.shape[1] // 2
        low, high = squares[:, :half], squares[:, half:]
        there = odd[level][:, :half]
        step = 2**level
        squares = jnp.where(there, high, low) + pltpu.roll(jnp.where(there, low, high), 8 - step, 0)
    return squares


def row_walsh(values, row_ids):
    for level in range(3):
        step = 2**level
        up, down = pltpu.roll(values, 8 - step, 0), pltpu.roll(values, step, 0)
        values = jnp.where((row_ids >> level) & 1 == 1, down - values, values + up)
    return values


def walsh_matrix():
    common = lax.broadcasted_iota(jnp.int32, (LANES, LANES), 0) & lax.broadcasted_iota(jnp.int32, (LANES, LANES), 1)
    parity = common ^ (common >> 4)
    parity = parity ^ (parity >> 2)
    parity = (parity ^ (parity >> 1)) & 1
    return (1 - 2 * parity).astype(jnp.float32).astype(jnp.bfloat16)


def walsh_over_first(values):
    count, *rest = values.shape
    for step in (4, 2, 1):
        pairs = values.reshape(count // (2 * step), 2, step, *rest)
        low, high = pairs[:, 0], pairs[:, 1]
        values = jnp.stack([low + high, low - high], axis=1).reshape(count, *rest)
    return values


def wait_for(slots, count, semaphore):
    pltpu.make_async_copy(slots.at[pl.ds(0, count)], slots.at[pl.ds(0, count)], semaphore).wait()


def exchange(
    amplitudes, qubit_order, out, lanes, lines,
    held, order, keep, give, got, own, sent, recv1, send2, recv2, load_sem, order_sem, twin_sem, far_sem, near_sem, sem2, seen,
):
    here = Places()

    barrier = pltpu.get_barrier_semaphore()
    for offset in GREETED:
        pl.semaphore_signal(barrier, inc=1, **here.at(offset))
    for z in range(NZ - 1, 0, -1):
        @pl.when(z > here.z)
        def _():
            pl.semaphore_signal(barrier, inc=1, **here.at_z(z))


    loads = []
    for part in range(NY):
        columns = pl.ds(part * CHUNK, CHUNK)
        loads.append(pltpu.make_async_copy(amplitudes.at[:, :, columns], held.at[:, :, columns], load_sem.at[part]))
    for load in loads:
        load.start()
    order_load = pltpu.make_async_copy(qubit_order, order, order_sem)
    order_load.start()
    row_ids = lax.broadcasted_iota(jnp.int32, (8, CHUNK // 4), 0)
    odd = [(row_ids >> level) & 1 == 1 for level in range(3)]
    core_sign = sign(here.k)
    mass = jnp.zeros((8, 2 * LANES), jnp.float32)
    for part in range(NY):
        loads[part].wait()
        real = held[0, :, part * CHUNK : (part + 1) * CHUNK]
        imag = held[1, :, part * CHUNK : (part + 1) * CHUNK]
        squares = real * real + imag * imag
        zero, one = rows_summed(squares[:, : CHUNK // 2], odd), rows_summed(squares[:, CHUNK // 2 :], odd)
        mass = mass + (zero + one)
        one = core_sign * one
        keep[part] = zero + one
        give[part] = zero - one
    own_part, other_part = walsh_over_first(keep[...]), walsh_over_first(give[0:NY])
    give[0:NY] = other_part
    own_mass = jnp.sum(mass[:, :LANES] + mass[:, LANES:], axis=0, keepdims=True)
    give[NY] = jnp.broadcast_to(jnp.concatenate([own_mass, own_mass], axis=1), (8, 2 * LANES))
    spread = jnp.broadcast_to(own_mass, (NY, 1, LANES))
    for which, part in enumerate((own_part, other_part)):
        for half in range(2):
            own[which, half, :, 0:8, :] = part[:, :, half * LANES : (half + 1) * LANES]
            own[which, half, :, 8:9, :] = spread

    pl.semaphore_wait(barrier, len(GREETED) + here.z)
    twin = pltpu.make_async_remote_copy(give, got, twin_sem.at[0], twin_sem.at[1], **here.at(TWIN))
    twin.start()
    sides = {0: here.pair_bit, PAIR: 1 - here.pair_bit}
    for offset in FAR:
        pltpu.make_async_remote_copy(
            own.at[offset[1], sides[offset[3]], here.ys[offset[0]]],
            recv1.at[SLOTS.index(offset)], far_sem.at[0], far_sem.at[1], **here.at(offset)
        ).start()
    for offset in ALONG_X:
        pl.semaphore_signal(seen.at[0], inc=1, **here.at(offset))
    for z in range(NZ - 1):
        @pl.when(z < here.z)
        def _():
            pl.semaphore_signal(seen.at[1], inc=1, **here.at_z(z))
    twin.wait_recv()

    mass = own_mass + got[NY, 0:1, :LANES]
    spread = jnp.broadcast_to(mass, (NY, 1, LANES))
    for half in range(2):
        columns = slice(half * LANES, (half + 1) * LANES)
        sent[half, :, 0:8, :] = own[0, half, :, 0:8, :] + got[0:NY, :, columns]
        sent[half, :, 8:9, :] = spread
    for offset in NEAR:
        pltpu.make_async_remote_copy(
            sent.at[sides[offset[3]], here.ys[offset[0]]],
            recv1.at[SLOTS.index(offset)], near_sem.at[0], near_sem.at[1], **here.at(offset)
        ).start()

    order_load.wait()
    lanes[...], lines[...] = sources(order)
    matrix = walsh_matrix()
    signs = [sign(lax.rem(lax.div(here.z, 2**level), 2)) for level in (2, 1, 0)] + [sign(lax.div(here.x, 2))]
    pair_sign = sign(here.pair_bit)
    wait_for(recv1, len(FAR), far_sem.at[1])
    wait_for(recv1, len(NEAR), near_sem.at[1])

    this_side = recv1[0:OWN_SIDE].sum(axis=0) + sent[here.pair_bit, here.y]
    that_side = recv1[OWN_SIDE:].sum(axis=0)
    send2[0] = this_side + that_side
    send2[1, 0:8, :] = pair_sign * (this_side[0:8] - that_side[0:8])
    send2[1, 8:9, :] = this_side[8:9] + that_side[8:9]

    pl.semaphore_wait(seen.at[0], len(ALONG_X))
    slot = here.z * NX + here.x
    bits = {dx: lax.rem(here.xs[dx], 2) for dx in range(NX)}
    for z in range(NZ):
        if z:
            @pl.when(here.z == z - 1)
            def _():
                pl.semaphore_wait(seen.at[1], NZ - z)
        for dx in (2, 1, 3, 0):
            height, pair = (pl.ds(0, ROWS), 0) if dx % 2 == 0 else (pl.ds(0, 8), 2)
            copy = pltpu.make_async_remote_copy(
                send2.at[bits[dx], height], recv2.at[slot, height], sem2.at[pair], sem2.at[pair + 1], **here.at_z(z, dx)
            )
            if dx:
                copy.start()
            else:
                pl.when(here.z != z)(copy.start)
    recv2[slot] = send2[here.pair_bit]
    light = recv2.at[pl.ds(0, NZ * NX // 2), pl.ds(0, 8)]
    wait_for(recv2, NZ * NX // 2 - 1, sem2.at[1])
    pltpu.make_async_copy(light, light, sem2.at[3]).wait()

    masses = functools.reduce(jnp.add, [recv2[2 * i + here.pair_bit, 8:9, :] for i in range(NZ * NX // 2)])
    terms = recv2[:, 0:8, :]
    for factor in signs:
        half = terms.shape[0] // 2
        terms = terms[:half] + factor * terms[half:]
    rows = row_ids[:, :LANES]
    values = jnp.concatenate(
        [
            row_walsh(terms[0] + terms[1], rows),
            row_walsh(terms[0] - terms[1], rows),
            jnp.broadcast_to(masses, (16, LANES)),
        ],
        axis=0,
    )
    high = values.astype(jnp.bfloat16)
    rest = values - high.astype(jnp.float32)
    middle = rest.astype(jnp.bfloat16)
    low = (rest - middle.astype(jnp.float32)).astype(jnp.bfloat16)
    product = jnp.dot(jnp.concatenate([high, middle, low], axis=0), matrix, preferred_element_type=jnp.float32)
    out[...] = product[0:24] + product[32:56] + product[64:88]
    twin.wait_send()
    wait_for(recv1, len(FAR), far_sem.at[0])
    wait_for(recv1, len(NEAR), near_sem.at[0])
    wait_for(recv2, NZ * NX // 2 - 1, sem2.at[0])
    pltpu.make_async_copy(light, light, sem2.at[2]).wait()


def sources(order):
    target = lax.broadcasted_iota(jnp.int32, (16, LANES), 0) * LANES + lax.broadcasted_iota(jnp.int32, (16, LANES), 1)
    source = jnp.zeros_like(target)
    for location in range(11):
        source = source + (((target >> location) & 1) << order[location])
    row = source >> 7
    return source & 127, ((row & 1) << 3) | ((row >> 3) & 1) | ((row >> 1) & 2) | ((row << 1) & 4)


def reorder(values, lanes, lines, out):
    lane, line = lanes[...], lines[...]
    result = jnp.zeros((16, LANES), jnp.float32)
    for i in range(16):
        row = jnp.broadcast_to(values[i : i + 1, :], (16, LANES))
        result = jnp.where(line == i, jnp.take_along_axis(row, lane, axis=1), result)
    total = jnp.broadcast_to(values[16:17, 0:1], (16, LANES))
    out[...] = result * 1024.0 / total


def local(amplitudes, qubit_order):
    vmem = pl.BlockSpec(memory_space=pltpu.VMEM)
    f32 = jnp.float32
    tables = pl.pallas_call(
        exchange,
        out_shape=[pltpu.VMEM((24, LANES), f32), pltpu.VMEM((16, LANES), jnp.int32), pltpu.VMEM((16, LANES), jnp.int32)],
        in_specs=[pl.BlockSpec(memory_space=pl.ANY), pl.BlockSpec(memory_space=pl.ANY)],
        out_specs=[vmem] * 3,
        scratch_shapes=[
            pltpu.VMEM((2, 8, NY * CHUNK), f32),
            pltpu.SMEM((11,), jnp.int32),
            pltpu.VMEM((NY, 8, 2 * LANES), f32),
            pltpu.VMEM((NY + 1, 8, 2 * LANES), f32),
            pltpu.VMEM((NY + 1, 8, 2 * LANES), f32),
            pltpu.VMEM((NK, 2, NY, ROWS, LANES), f32),
            pltpu.VMEM((2, NY, ROWS, LANES), f32),
            pltpu.VMEM((len(SLOTS), ROWS, LANES), f32),
            pltpu.VMEM((2, ROWS, LANES), f32),
            pltpu.VMEM((NZ * NX, ROWS, LANES), f32),
            pltpu.SemaphoreType.DMA((NY,)),
            pltpu.SemaphoreType.DMA,
            pltpu.SemaphoreType.DMA((2,)),
            pltpu.SemaphoreType.DMA((2,)),
            pltpu.SemaphoreType.DMA((2,)),
            pltpu.SemaphoreType.DMA((4,)),
            pltpu.SemaphoreType.REGULAR((2,)),
        ],
        compiler_params=pltpu.CompilerParams(
            collective_id=0, has_side_effects=True, vmem_limit_bytes=56 * 2**20
        ),
    )(amplitudes, qubit_order)
    result = pl.pallas_call(
        reorder,
        out_shape=jax.ShapeDtypeStruct((16, LANES), f32),
        in_specs=[vmem] * 3,
        out_specs=vmem,
    )(*(pltpu.with_memory_space_constraint(table, pltpu.VMEM) for table in tables))
    return result.reshape(1, -1)


def solution(mesh):
    return jax.shard_map(
        local, mesh=mesh, in_specs=(P(None, "row", "col"), P()), out_specs=P("col", "row"), check_vma=False
    )
```

```python
import functools
import itertools

import jax
import jax.numpy as jnp
from jax import lax
from jax.experimental import pallas as pl
from jax.experimental.pallas import tpu as pltpu
from jax.sharding import PartitionSpec as P

NY, NK, NZ, NX = 8, 2, 8, 4
CHUNK = 4096
LANES = 128
ROWS = 9
PAIR = "pair"


def hops(offset):
    dy, dk, dz, dx = offset
    dx = 1 if dx == PAIR else min(dx, NX - dx)
    return min(dy, NY - dy) + min(dz, NZ - dz) + dx


def far_first(offsets):
    return sorted((o for o in offsets if o != (0, 0, 0, 0)), key=lambda o: -hops(o))


TWIN = (0, 1, 0, 0)
FAR_Y = (4,)
FAR = far_first(itertools.product(FAR_Y, range(NK), (0,), (0, PAIR)))
NEAR = far_first(o for o in itertools.product(range(NY), (0,), (0,), (0, PAIR)) if o[0] not in FAR_Y)
SLOTS = sorted(FAR + NEAR, key=lambda o: o[3] == PAIR)
OWN_SIDE = sum(o[3] != PAIR for o in SLOTS)
ALONG_X = far_first(itertools.product((0,), (0,), (0,), range(NX)))
GREETED = far_first({o for o in FAR + NEAR if o != (0, 0, 0, PAIR)} | set(ALONG_X) | {TWIN})


class Places:
    def __init__(self):
        row, col = lax.axis_index("row"), lax.axis_index("col")
        self.y, self.k = lax.div(row, 2), lax.rem(row, 2)
        self.z, self.x = lax.div(col, NX), lax.rem(col, NX)
        self.pair_bit = lax.rem(self.x, 2)
        self.ys = [self.y] + [lax.rem(self.y + i, NY) for i in range(1, NY)]
        self.zs = [self.z] + [lax.rem(self.z + i, NZ) for i in range(1, NZ)]
        self.xs = {i: lax.rem(self.x + i, NX) for i in range(1, NX)} | {0: self.x, PAIR: self.x + 1 - 2 * self.pair_bit}
        other = 1 - self.k
        self.row = {(i, j): self.ys[i] * NK + (other if j else self.k) for i in range(NY) for j in range(NK)}
        self.col = {(i, j): self.zs[i] * NX + self.xs[j] for i in range(NZ) for j in range(NX)}
        self.col[0, PAIR] = self.z * NX + self.xs[PAIR]

    def at_z(self, z, dx=0):
        return {
            "device_id": (self.row[0, 0], z * NX + self.xs[dx]),
            "device_id_type": pl.DeviceIdType.MESH,
        }

    def at(self, offset):
        dy, dk, dz, dx = offset
        return {
            "device_id": (self.row[dy, dk], self.col[dz, dx]),
            "device_id_type": pl.DeviceIdType.MESH,
        }


def sign(bit):
    return (1 - 2 * bit).astype(jnp.float32)


def rows_summed(squares, odd):
    for level in range(3):
        half = squares.shape[1] // 2
        low, high = squares[:, :half], squares[:, half:]
        there = odd[level][:, :half]
        step = 2**level
        squares = jnp.where(there, high, low) + pltpu.roll(jnp.where(there, low, high), 8 - step, 0)
    return squares


def row_walsh(values, row_ids):
    for level in range(3):
        step = 2**level
        up, down = pltpu.roll(values, 8 - step, 0), pltpu.roll(values, step, 0)
        values = jnp.where((row_ids >> level) & 1 == 1, down - values, values + up)
    return values


def walsh_matrix():
    common = lax.broadcasted_iota(jnp.int32, (LANES, LANES), 0) & lax.broadcasted_iota(jnp.int32, (LANES, LANES), 1)
    parity = common ^ (common >> 4)
    parity = parity ^ (parity >> 2)
    parity = (parity ^ (parity >> 1)) & 1
    return (1 - 2 * parity).astype(jnp.float32).astype(jnp.bfloat16)


def walsh_over_first(values):
    count, *rest = values.shape
    for step in (4, 2, 1):
        pairs = values.reshape(count // (2 * step), 2, step, *rest)
        low, high = pairs[:, 0], pairs[:, 1]
        values = jnp.stack([low + high, low - high], axis=1).reshape(count, *rest)
    return values


def wait_for(slots, count, semaphore):
    pltpu.make_async_copy(slots.at[pl.ds(0, count)], slots.at[pl.ds(0, count)], semaphore).wait()


def exchange(
    amplitudes, qubit_order, out, lanes, lines,
    held, order, keep, give, got, own, sent, recv1, send2, recv2, load_sem, order_sem, twin_sem, far_sem, near_sem, sem2, seen,
):
    here = Places()

    loads = []
    for part in range(NY):
        columns = pl.ds(part * CHUNK, CHUNK)
        loads.append(pltpu.make_async_copy(amplitudes.at[:, :, columns], held.at[:, :, columns], load_sem.at[part]))
    for load in loads:
        load.start()
    order_load = pltpu.make_async_copy(qubit_order, order, order_sem)
    order_load.start()
    barrier = pltpu.get_barrier_semaphore()
    for offset in GREETED:
        pl.semaphore_signal(barrier, inc=1, **here.at(offset))
    for z in range(NZ - 1, 0, -1):
        @pl.when(z > here.z)
        def _():
            pl.semaphore_signal(barrier, inc=1, **here.at_z(z))

    row_ids = lax.broadcasted_iota(jnp.int32, (8, CHUNK // 4), 0)
    odd = [(row_ids >> level) & 1 == 1 for level in range(3)]
    core_sign = sign(here.k)
    mass = jnp.zeros((8, 2 * LANES), jnp.float32)
    for part in range(NY):
        loads[part].wait()
        real = held[0, :, part * CHUNK : (part + 1) * CHUNK]
        imag = held[1, :, part * CHUNK : (part + 1) * CHUNK]
        squares = real * real + imag * imag
        zero, one = rows_summed(squares[:, : CHUNK // 2], odd), rows_summed(squares[:, CHUNK // 2 :], odd)
        mass = mass + (zero + one)
        one = core_sign * one
        keep[part] = zero + one
        give[part] = zero - one
    own_part, other_part = walsh_over_first(keep[...]), walsh_over_first(give[0:NY])
    give[0:NY] = other_part
    give[NY] = mass
    own_mass = jnp.sum(mass[:, :LANES] + mass[:, LANES:], axis=0, keepdims=True)
    spread = jnp.broadcast_to(own_mass, (NY, 1, LANES))
    for which, part in enumerate((own_part, other_part)):
        for half in range(2):
            own[which, half, :, 0:8, :] = part[:, :, half * LANES : (half + 1) * LANES]
            own[which, half, :, 8:9, :] = spread

    pl.semaphore_wait(barrier, len(GREETED) + here.z)
    twin = pltpu.make_async_remote_copy(give, got, twin_sem.at[0], twin_sem.at[1], **here.at(TWIN))
    twin.start()
    sides = {0: here.pair_bit, PAIR: 1 - here.pair_bit}
    for offset in FAR:
        pltpu.make_async_remote_copy(
            own.at[offset[1], sides[offset[3]], here.ys[offset[0]]],
            recv1.at[SLOTS.index(offset)], far_sem.at[0], far_sem.at[1], **here.at(offset)
        ).start()
    for offset in ALONG_X:
        pl.semaphore_signal(seen.at[0], inc=1, **here.at(offset))
    for z in range(NZ - 1):
        @pl.when(z < here.z)
        def _():
            pl.semaphore_signal(seen.at[1], inc=1, **here.at_z(z))
    twin.wait_recv()

    mass = own_mass + jnp.sum(got[NY, :, :LANES] + got[NY, :, LANES:], axis=0, keepdims=True)
    spread = jnp.broadcast_to(mass, (NY, 1, LANES))
    for half in range(2):
        columns = slice(half * LANES, (half + 1) * LANES)
        sent[half, :, 0:8, :] = own[0, half, :, 0:8, :] + got[0:NY, :, columns]
        sent[half, :, 8:9, :] = spread
    for offset in NEAR:
        pltpu.make_async_remote_copy(
            sent.at[sides[offset[3]], here.ys[offset[0]]],
            recv1.at[SLOTS.index(offset)], near_sem.at[0], near_sem.at[1], **here.at(offset)
        ).start()

    order_load.wait()
    lanes[...], lines[...] = sources(order)
    matrix = walsh_matrix()
    signs = [sign(lax.rem(lax.div(here.z, 2**level), 2)) for level in (2, 1, 0)] + [sign(lax.div(here.x, 2))]
    pair_sign = sign(here.pair_bit)
    pl.semaphore_wait(seen.at[0], len(ALONG_X))
    slot = here.z * NX + here.x
    bits = {dx: lax.rem(here.xs[dx], 2) for dx in range(NX)}
    wait_for(recv1, len(FAR), far_sem.at[1])
    wait_for(recv1, len(NEAR), near_sem.at[1])

    this_side = recv1[0:OWN_SIDE].sum(axis=0) + sent[here.pair_bit, here.y]
    that_side = recv1[OWN_SIDE:].sum(axis=0)
    send2[0] = this_side + that_side
    send2[1, 0:8, :] = pair_sign * (this_side[0:8] - that_side[0:8])
    send2[1, 8:9, :] = this_side[8:9] + that_side[8:9]

    for z in range(NZ):
        if z:
            @pl.when(here.z == z - 1)
            def _():
                pl.semaphore_wait(seen.at[1], NZ - z)
        for dx in (2, 1, 3, 0):
            height, pair = (pl.ds(0, ROWS), 0) if dx % 2 == 0 else (pl.ds(0, 8), 2)
            copy = pltpu.make_async_remote_copy(
                send2.at[bits[dx], height], recv2.at[slot, height], sem2.at[pair], sem2.at[pair + 1], **here.at_z(z, dx)
            )
            if dx:
                copy.start()
            else:
                pl.when(here.z != z)(copy.start)
    recv2[slot] = send2[here.pair_bit]
    light = recv2.at[pl.ds(0, NZ * NX // 2), pl.ds(0, 8)]
    wait_for(recv2, NZ * NX // 2 - 1, sem2.at[1])
    pltpu.make_async_copy(light, light, sem2.at[3]).wait()

    masses = functools.reduce(jnp.add, [recv2[2 * i + here.pair_bit, 8:9, :] for i in range(NZ * NX // 2)])
    terms = recv2[:, 0:8, :]
    for factor in signs:
        half = terms.shape[0] // 2
        terms = terms[:half] + factor * terms[half:]
    rows = row_ids[:, :LANES]
    values = jnp.concatenate(
        [
            row_walsh(terms[0] + terms[1], rows),
            row_walsh(terms[0] - terms[1], rows),
            jnp.broadcast_to(masses, (16, LANES)),
        ],
        axis=0,
    )
    high = values.astype(jnp.bfloat16)
    rest = values - high.astype(jnp.float32)
    middle = rest.astype(jnp.bfloat16)
    low = (rest - middle.astype(jnp.float32)).astype(jnp.bfloat16)
    product = jnp.dot(jnp.concatenate([high, middle, low], axis=0), matrix, preferred_element_type=jnp.float32)
    out[...] = product[0:24] + product[32:56] + product[64:88]
    twin.wait_send()
    wait_for(recv1, len(FAR), far_sem.at[0])
    wait_for(recv1, len(NEAR), near_sem.at[0])
    wait_for(recv2, NZ * NX // 2 - 1, sem2.at[0])
    pltpu.make_async_copy(light, light, sem2.at[2]).wait()


def sources(order):
    target = lax.broadcasted_iota(jnp.int32, (16, LANES), 0) * LANES + lax.broadcasted_iota(jnp.int32, (16, LANES), 1)
    source = jnp.zeros_like(target)
    for location in range(11):
        source = source + (((target >> location) & 1) << order[location])
    row = source >> 7
    return source & 127, ((row & 1) << 3) | ((row >> 3) & 1) | ((row >> 1) & 2) | ((row << 1) & 4)


def reorder(values, lanes, lines, out):
    lane, line = lanes[...], lines[...]
    result = jnp.zeros((16, LANES), jnp.float32)
    for i in range(16):
        row = jnp.broadcast_to(values[i : i + 1, :], (16, LANES))
        result = jnp.where(line == i, jnp.take_along_axis(row, lane, axis=1), result)
    total = jnp.broadcast_to(values[16:17, 0:1], (16, LANES))
    out[...] = result * 1024.0 / total


def local(amplitudes, qubit_order):
    vmem = pl.BlockSpec(memory_space=pltpu.VMEM)
    f32 = jnp.float32
    tables = pl.pallas_call(
        exchange,
        out_shape=[pltpu.VMEM((24, LANES), f32), pltpu.VMEM((16, LANES), jnp.int32), pltpu.VMEM((16, LANES), jnp.int32)],
        in_specs=[pl.BlockSpec(memory_space=pl.ANY), pl.BlockSpec(memory_space=pl.ANY)],
        out_specs=[vmem] * 3,
        scratch_shapes=[
            pltpu.VMEM((2, 8, NY * CHUNK), f32),
            pltpu.SMEM((11,), jnp.int32),
            pltpu.VMEM((NY, 8, 2 * LANES), f32),
            pltpu.VMEM((NY + 1, 8, 2 * LANES), f32),
            pltpu.VMEM((NY + 1, 8, 2 * LANES), f32),
            pltpu.VMEM((NK, 2, NY, ROWS, LANES), f32),
            pltpu.VMEM((2, NY, ROWS, LANES), f32),
            pltpu.VMEM((len(SLOTS), ROWS, LANES), f32),
            pltpu.VMEM((2, ROWS, LANES), f32),
            pltpu.VMEM((NZ * NX, ROWS, LANES), f32),
            pltpu.SemaphoreType.DMA((NY,)),
            pltpu.SemaphoreType.DMA,
            pltpu.SemaphoreType.DMA((2,)),
            pltpu.SemaphoreType.DMA((2,)),
            pltpu.SemaphoreType.DMA((2,)),
            pltpu.SemaphoreType.DMA((4,)),
            pltpu.SemaphoreType.REGULAR((2,)),
        ],
        compiler_params=pltpu.CompilerParams(
            collective_id=0, has_side_effects=True, vmem_limit_bytes=56 * 2**20
        ),
    )(amplitudes, qubit_order)
    result = pl.pallas_call(
        reorder,
        out_shape=jax.ShapeDtypeStruct((16, LANES), f32),
        in_specs=[vmem] * 3,
        out_specs=vmem,
    )(*(pltpu.with_memory_space_constraint(table, pltpu.VMEM) for table in tables))
    return result.reshape(1, -1)


def solution(mesh):
    return jax.shard_map(
        local, mesh=mesh, in_specs=(P(None, "row", "col"), P()), out_specs=P("col", "row"), check_vma=False
    )
```

```python
import functools
import itertools

import jax
import jax.numpy as jnp
from jax import lax
from jax.experimental import pallas as pl
from jax.experimental.pallas import tpu as pltpu
from jax.sharding import PartitionSpec as P

NY, NK, NZ, NX = 8, 2, 8, 4
CHUNK = 4096
LANES = 128
ROWS = 9
PAIR = "pair"


def hops(offset):
    dy, dk, dz, dx = offset
    dx = 1 if dx == PAIR else min(dx, NX - dx)
    return min(dy, NY - dy) + min(dz, NZ - dz) + dx


def far_first(offsets):
    return sorted((o for o in offsets if o != (0, 0, 0, 0)), key=lambda o: -hops(o))


TWIN = (0, 1, 0, 0)
FAR_Y = (4,)
FAR = far_first(itertools.product(FAR_Y, range(NK), (0,), (0, PAIR)))
NEAR = far_first(o for o in itertools.product(range(NY), (0,), (0,), (0, PAIR)) if o[0] not in FAR_Y)
SLOTS = sorted(FAR + NEAR, key=lambda o: o[3] == PAIR)
OWN_SIDE = sum(o[3] != PAIR for o in SLOTS)
ALONG_X = far_first(itertools.product((0,), (0,), (0,), range(NX)))
GREETED = far_first({o for o in FAR + NEAR if o != (0, 0, 0, PAIR)} | set(ALONG_X) | {TWIN})


class Places:
    def __init__(self):
        row, col = lax.axis_index("row"), lax.axis_index("col")
        self.y, self.k = lax.div(row, 2), lax.rem(row, 2)
        self.z, self.x = lax.div(col, NX), lax.rem(col, NX)
        self.pair_bit = lax.rem(self.x, 2)
        self.ys = [self.y] + [lax.rem(self.y + i, NY) for i in range(1, NY)]
        self.zs = [self.z] + [lax.rem(self.z + i, NZ) for i in range(1, NZ)]
        self.xs = {i: lax.rem(self.x + i, NX) for i in range(1, NX)} | {0: self.x, PAIR: self.x + 1 - 2 * self.pair_bit}
        other = 1 - self.k
        self.row = {(i, j): self.ys[i] * NK + (other if j else self.k) for i in range(NY) for j in range(NK)}
        self.col = {(i, j): self.zs[i] * NX + self.xs[j] for i in range(NZ) for j in range(NX)}
        self.col[0, PAIR] = self.z * NX + self.xs[PAIR]

    def at_z(self, z, dx=0):
        return {
            "device_id": (self.row[0, 0], z * NX + self.xs[dx]),
            "device_id_type": pl.DeviceIdType.MESH,
        }

    def at(self, offset):
        dy, dk, dz, dx = offset
        return {
            "device_id": (self.row[dy, dk], self.col[dz, dx]),
            "device_id_type": pl.DeviceIdType.MESH,
        }


def sign(bit):
    return (1 - 2 * bit).astype(jnp.float32)


def rows_summed(squares, odd):
    for level in range(3):
        half = squares.shape[1] // 2
        low, high = squares[:, :half], squares[:, half:]
        there = odd[level][:, :half]
        step = 2**level
        squares = jnp.where(there, high, low) + pltpu.roll(jnp.where(there, low, high), 8 - step, 0)
    return squares


def row_walsh(values, row_ids):
    for level in range(3):
        step = 2**level
        up, down = pltpu.roll(values, 8 - step, 0), pltpu.roll(values, step, 0)
        values = jnp.where((row_ids >> level) & 1 == 1, down - values, values + up)
    return values


def walsh_matrix():
    common = lax.broadcasted_iota(jnp.int32, (LANES, LANES), 0) & lax.broadcasted_iota(jnp.int32, (LANES, LANES), 1)
    parity = common ^ (common >> 4)
    parity = parity ^ (parity >> 2)
    parity = (parity ^ (parity >> 1)) & 1
    return (1 - 2 * parity).astype(jnp.float32).astype(jnp.bfloat16)


def walsh_over_first(values):
    count, *rest = values.shape
    for step in (4, 2, 1):
        pairs = values.reshape(count // (2 * step), 2, step, *rest)
        low, high = pairs[:, 0], pairs[:, 1]
        values = jnp.stack([low + high, low - high], axis=1).reshape(count, *rest)
    return values


def wait_for(slots, count, semaphore):
    pltpu.make_async_copy(slots.at[pl.ds(0, count)], slots.at[pl.ds(0, count)], semaphore).wait()


def exchange(
    amplitudes, qubit_order, out, lanes, lines,
    held, order, keep, give, got, own, sent, recv1, send2, recv2, load_sem, order_sem, twin_sem, far_sem, near_sem, sem2, seen,
):
    here = Places()

    loads = []
    for part in range(NY):
        columns = pl.ds(part * CHUNK, CHUNK)
        loads.append(pltpu.make_async_copy(amplitudes.at[:, :, columns], held.at[:, :, columns], load_sem.at[part]))
    for load in loads:
        load.start()
    order_load = pltpu.make_async_copy(qubit_order, order, order_sem)
    order_load.start()
    barrier = pltpu.get_barrier_semaphore()
    for offset in GREETED:
        pl.semaphore_signal(barrier, inc=1, **here.at(offset))
    for z in range(NZ - 1, 0, -1):
        @pl.when(z > here.z)
        def _():
            pl.semaphore_signal(barrier, inc=1, **here.at_z(z))

    row_ids = lax.broadcasted_iota(jnp.int32, (8, CHUNK // 4), 0)
    odd = [(row_ids >> level) & 1 == 1 for level in range(3)]
    core_sign = sign(here.k)
    mass = jnp.zeros((8, 2 * LANES), jnp.float32)
    for part in range(NY):
        loads[part].wait()
        real = held[0, :, part * CHUNK : (part + 1) * CHUNK]
        imag = held[1, :, part * CHUNK : (part + 1) * CHUNK]
        squares = real * real + imag * imag
        zero, one = rows_summed(squares[:, : CHUNK // 2], odd), rows_summed(squares[:, CHUNK // 2 :], odd)
        mass = mass + (zero + one)
        one = core_sign * one
        keep[part] = zero + one
        give[part] = zero - one
    own_part, other_part = walsh_over_first(keep[...]), walsh_over_first(give[0:NY])
    give[0:NY] = other_part
    own_mass = jnp.sum(mass[:, :LANES] + mass[:, LANES:], axis=0, keepdims=True)
    give[NY] = jnp.broadcast_to(jnp.concatenate([own_mass, own_mass], axis=1), (8, 2 * LANES))
    spread = jnp.broadcast_to(own_mass, (NY, 1, LANES))
    for which, part in enumerate((own_part, other_part)):
        for half in range(2):
            own[which, half, :, 0:8, :] = part[:, :, half * LANES : (half + 1) * LANES]
            own[which, half, :, 8:9, :] = spread

    pl.semaphore_wait(barrier, len(GREETED) + here.z)
    twin = pltpu.make_async_remote_copy(give, got, twin_sem.at[0], twin_sem.at[1], **here.at(TWIN))
    twin.start()
    sides = {0: here.pair_bit, PAIR: 1 - here.pair_bit}
    for offset in FAR:
        pltpu.make_async_remote_copy(
            own.at[offset[1], sides[offset[3]], here.ys[offset[0]]],
            recv1.at[SLOTS.index(offset)], far_sem.at[0], far_sem.at[1], **here.at(offset)
        ).start()
    for offset in ALONG_X:
        pl.semaphore_signal(seen.at[0], inc=1, **here.at(offset))
    for z in range(NZ - 1):
        @pl.when(z < here.z)
        def _():
            pl.semaphore_signal(seen.at[1], inc=1, **here.at_z(z))
    twin.wait_recv()

    mass = own_mass + got[NY, 0:1, :LANES]
    spread = jnp.broadcast_to(mass, (NY, 1, LANES))
    for half in range(2):
        columns = slice(half * LANES, (half + 1) * LANES)
        sent[half, :, 0:8, :] = own[0, half, :, 0:8, :] + got[0:NY, :, columns]
        sent[half, :, 8:9, :] = spread
    for offset in NEAR:
        pltpu.make_async_remote_copy(
            sent.at[sides[offset[3]], here.ys[offset[0]]],
            recv1.at[SLOTS.index(offset)], near_sem.at[0], near_sem.at[1], **here.at(offset)
        ).start()

    order_load.wait()
    lanes[...], lines[...] = sources(order)
    matrix = walsh_matrix()
    signs = [sign(lax.rem(lax.div(here.z, 2**level), 2)) for level in (2, 1, 0)] + [sign(lax.div(here.x, 2))]
    pair_sign = sign(here.pair_bit)
    pl.semaphore_wait(seen.at[0], len(ALONG_X))
    slot = here.z * NX + here.x
    bits = {dx: lax.rem(here.xs[dx], 2) for dx in range(NX)}
    wait_for(recv1, len(FAR), far_sem.at[1])
    wait_for(recv1, len(NEAR), near_sem.at[1])

    this_side = recv1[0:OWN_SIDE].sum(axis=0) + sent[here.pair_bit, here.y]
    that_side = recv1[OWN_SIDE:].sum(axis=0)
    send2[0] = this_side + that_side
    send2[1, 0:8, :] = pair_sign * (this_side[0:8] - that_side[0:8])
    send2[1, 8:9, :] = this_side[8:9] + that_side[8:9]

    for z in range(NZ):
        if z:
            @pl.when(here.z == z - 1)
            def _():
                pl.semaphore_wait(seen.at[1], NZ - z)
        for dx in (2, 1, 3, 0):
            height, pair = (pl.ds(0, ROWS), 0) if dx % 2 == 0 else (pl.ds(0, 8), 2)
            copy = pltpu.make_async_remote_copy(
                send2.at[bits[dx], height], recv2.at[slot, height], sem2.at[pair], sem2.at[pair + 1], **here.at_z(z, dx)
            )
            if dx:
                copy.start()
            else:
                pl.when(here.z != z)(copy.start)
    recv2[slot] = send2[here.pair_bit]
    light = recv2.at[pl.ds(0, NZ * NX // 2), pl.ds(0, 8)]
    wait_for(recv2, NZ * NX // 2 - 1, sem2.at[1])
    pltpu.make_async_copy(light, light, sem2.at[3]).wait()

    masses = functools.reduce(jnp.add, [recv2[2 * i + here.pair_bit, 8:9, :] for i in range(NZ * NX // 2)])
    terms = recv2[:, 0:8, :]
    for factor in signs:
        half = terms.shape[0] // 2
        terms = terms[:half] + factor * terms[half:]
    rows = row_ids[:, :LANES]
    values = jnp.concatenate(
        [
            row_walsh(terms[0] + terms[1], rows),
            row_walsh(terms[0] - terms[1], rows),
            jnp.broadcast_to(masses, (16, LANES)),
        ],
        axis=0,
    )
    high = values.astype(jnp.bfloat16)
    rest = values - high.astype(jnp.float32)
    middle = rest.astype(jnp.bfloat16)
    low = (rest - middle.astype(jnp.float32)).astype(jnp.bfloat16)
    product = jnp.dot(jnp.concatenate([high, middle, low], axis=0), matrix, preferred_element_type=jnp.float32)
    out[...] = product[0:24] + product[32:56] + product[64:88]
    twin.wait_send()
    wait_for(recv1, len(FAR), far_sem.at[0])
    wait_for(recv1, len(NEAR), near_sem.at[0])
    wait_for(recv2, NZ * NX // 2 - 1, sem2.at[0])
    pltpu.make_async_copy(light, light, sem2.at[2]).wait()


def sources(order):
    target = lax.broadcasted_iota(jnp.int32, (16, LANES), 0) * LANES + lax.broadcasted_iota(jnp.int32, (16, LANES), 1)
    source = jnp.zeros_like(target)
    for location in range(11):
        source = source + (((target >> location) & 1) << order[location])
    row = source >> 7
    return source & 127, ((row & 1) << 3) | ((row >> 3) & 1) | ((row >> 1) & 2) | ((row << 1) & 4)


def reorder(values, lanes, lines, out):
    lane, line = lanes[...], lines[...]
    result = jnp.zeros((16, LANES), jnp.float32)
    for i in range(16):
        row = jnp.broadcast_to(values[i : i + 1, :], (16, LANES))
        result = jnp.where(line == i, jnp.take_along_axis(row, lane, axis=1), result)
    total = jnp.broadcast_to(values[16:17, 0:1], (16, LANES))
    out[...] = result * 1024.0 / total


def local(amplitudes, qubit_order):
    vmem = pl.BlockSpec(memory_space=pltpu.VMEM)
    f32 = jnp.float32
    tables = pl.pallas_call(
        exchange,
        out_shape=[pltpu.VMEM((24, LANES), f32), pltpu.VMEM((16, LANES), jnp.int32), pltpu.VMEM((16, LANES), jnp.int32)],
        in_specs=[pl.BlockSpec(memory_space=pl.ANY), pl.BlockSpec(memory_space=pl.ANY)],
        out_specs=[vmem] * 3,
        scratch_shapes=[
            pltpu.VMEM((2, 8, NY * CHUNK), f32),
            pltpu.SMEM((11,), jnp.int32),
            pltpu.VMEM((NY, 8, 2 * LANES), f32),
            pltpu.VMEM((NY + 1, 8, 2 * LANES), f32),
            pltpu.VMEM((NY + 1, 8, 2 * LANES), f32),
            pltpu.VMEM((NK, 2, NY, ROWS, LANES), f32),
            pltpu.VMEM((2, NY, ROWS, LANES), f32),
            pltpu.VMEM((len(SLOTS), ROWS, LANES), f32),
            pltpu.VMEM((2, ROWS, LANES), f32),
            pltpu.VMEM((NZ * NX, ROWS, LANES), f32),
            pltpu.SemaphoreType.DMA((NY,)),
            pltpu.SemaphoreType.DMA,
            pltpu.SemaphoreType.DMA((2,)),
            pltpu.SemaphoreType.DMA((2,)),
            pltpu.SemaphoreType.DMA((2,)),
            pltpu.SemaphoreType.DMA((4,)),
            pltpu.SemaphoreType.REGULAR((2,)),
        ],
        compiler_params=pltpu.CompilerParams(
            collective_id=0, has_side_effects=True, vmem_limit_bytes=56 * 2**20
        ),
    )(amplitudes, qubit_order)
    result = pl.pallas_call(
        reorder,
        out_shape=jax.ShapeDtypeStruct((16, LANES), f32),
        in_specs=[vmem] * 3,
        out_specs=vmem,
    )(*(pltpu.with_memory_space_constraint(table, pltpu.VMEM) for table in tables))
    return result.reshape(1, -1)


def solution(mesh):
    return jax.shard_map(
        local, mesh=mesh, in_specs=(P(None, "row", "col"), P()), out_specs=P("col", "row"), check_vma=False
    )
```
